256 devices in a mesh: dp: 32 (over z_lo, y, x), tensor: 8 (over z_hi, core).
Axes of the slice: x: 4, y: 4, z: 8 (z_hi: 4, z_lo: 2; z = z_hi * 2 + z_lo), core: 2. Of those that a mesh axis runs over, the one named last changes fastest.
Arguments:
- gradients: bfloat16 [5, 4608, 36864], P(None, 'dp', 'tensor'), may hold values from -6 to 6
- old_projectors: bfloat16 [5, 4608, 256], P(None, 'dp'), may hold values from -0.09375 to 0.09375
- sketches: bfloat16 [2, 36864, 256], P(None, 'tensor'), may hold values from -0.03125 to 0.03125
- refresh_order: int32 [5], replicated, may hold values from 0 to 4, each once
Outputs:
- projected: float32 [5, 36864, 256], P(None, ('tensor', 'dp'))
- new_projectors: bfloat16 [2, 4608, 256], P(None, 'dp')
The draws below stay inside these ranges and needn't reach their ends.
Inputs may be any that keep to these rules, and one draw needn't show every extreme that they name: `refresh_order`: each layer appears once; the first 2 entries name the refreshed layers.
All inputs are finite; a program needn't handle non-finite values.
Results may differ from the reference program's by a relative error of at most 0.002.
Values may be sent and summed in bfloat16 or wider, within the bound.
A program may use at most 128 MiB of HBM per device.

```python
import jax
import jax.numpy as jnp
from jax import lax

D = 4608
FF = 36864
RANK = 256
LAYERS = 5
REFRESH = 2


def raised(drawn, stream_key, source, target, parts, factor):
    def block_of(axis_at):
        return (jnp.arange(drawn.shape[axis_at]) // (drawn.shape[axis_at] // parts)).reshape((-1,) + (1,) * (drawn.ndim - 1 - axis_at))

    first = jax.random.permutation(stream_key, parts)[block_of(target)]
    far = (block_of(target) + parts // 2) % parts
    return jnp.where((block_of(source) == first) | (block_of(source) == far), factor * drawn, drawn)


def levels(own_key, shape, pieces, least, largest):
    def one(dim, shards_of):
        heights = jax.random.uniform(jax.random.fold_in(jax.random.fold_in(own_key, 6), dim), (shards_of,), jnp.float32, least / len(pieces), largest / len(pieces))
        return jnp.repeat(jnp.exp(heights), shape[dim] // shards_of).reshape((-1,) + (1,) * (len(shape) - dim - 1))

    gain = one(*pieces[0])
    for cut in pieces[1:]:
        gain = gain * one(*cut)
    return gain


def centred(own_key, extent, spread, most, shards=(), held_as=jnp.bfloat16):
    gain = levels(own_key, extent, shards, -0.22, 0.18) if shards else 1.0
    array = jax.random.normal(own_key, extent, jnp.float32) * spread * gain
    return jnp.minimum(jnp.maximum(array, -most), most).astype(held_as)


def noise_with(rng, shape, spread, bound, pieces, heavy, dtype=jnp.bfloat16):
    drawn = spread * jax.random.normal(rng, shape, jnp.float32)
    if pieces:
        drawn = drawn * levels(rng, shape, pieces, -0.22, 0.18)
    return jnp.clip(raised(drawn, jax.random.fold_in(rng, 3), *heavy), -bound, bound).astype(dtype)


def setup_inputs(seed: int = 0) -> dict:
    keys = jax.random.split(jax.random.key(seed), 5)
    gradients = noise_with(keys[0], (LAYERS, D, FF), 1.0, 6.0, ((1, 32), (2, 8)), (1, 2, 32, 2.75))
    old_projectors = centred(keys[1], (LAYERS, D, RANK), D ** -0.5, 0.09375, ((1, 32),))
    sketches = centred(keys[2], (REFRESH, FF, RANK), FF ** -0.5, 0.03125, ((1, 8),))
    refresh_order = jax.random.permutation(keys[3], LAYERS).astype(jnp.int32)
    return {"gradients": gradients, "old_projectors": old_projectors, "sketches": sketches, "refresh_order": refresh_order}


def reference(gradients, old_projectors, sketches, refresh_order):
    projectors = old_projectors
    fresh_list = []
    for index in range(REFRESH):
        layer_id = refresh_order[index].astype(jnp.int32)
        grad_full = lax.dynamic_index_in_dim(gradients, layer_id, 0, keepdims=False)
        sketch = jnp.dot(grad_full.astype(jnp.float32), sketches[index].astype(jnp.float32), preferred_element_type=jnp.float32)
        gram_sum = jnp.dot(sketch.T, sketch, precision=lax.Precision.HIGHEST)
        factor = jnp.linalg.cholesky(gram_sum)
        basis = lax.linalg.triangular_solve(factor, sketch, left_side=False, lower=True, transpose_a=True)
        fresh = basis.astype(jnp.bfloat16)
        fresh_list.append(fresh)
        projectors = lax.dynamic_update_index_in_dim(projectors, fresh, layer_id, 0)

    def project_layer(pair):
        grad_full, proj_full = pair
        return lax.dot_general(grad_full.astype(jnp.float32), proj_full.astype(jnp.float32), (((0,), (0,)), ((), ())), preferred_element_type=jnp.float32)
    projected = lax.map(project_layer, (gradients, projectors))
    return (projected, jnp.stack(fresh_list))
```

```python
import jax
import jax.numpy as jnp
from jax import lax
from jax.experimental import pallas as pl
from jax.experimental.pallas import tpu as pltpu
from jax.sharding import PartitionSpec as P

MESH = pl.DeviceIdType.MESH
HIGHEST = lax.Precision.HIGHEST
F32 = jnp.float32
BF16 = jnp.bfloat16

ROWS = 144
COLS = 4608
HALF = COLS // 2
RANK = 256
LAYERS = 5
FRESH = 2
LEAF = 64


def matmul(a, b):
    return jnp.dot(a, b, precision=HIGHEST, preferred_element_type=F32)


def matmul_nt(a, b):
    return lax.dot_general(a, b, (((1,), (1,)), ((), ())), precision=HIGHEST, preferred_element_type=F32)


def leaf_inverse(a):
    row_id = lax.broadcasted_iota(jnp.int32, (LEAF, 2 * LEAF), 0)
    lane_id = lax.broadcasted_iota(jnp.int32, (LEAF, 2 * LEAF), 1)
    eye = (lane_id[:, :LEAF] == row_id[:, :LEAF]).astype(F32)
    m = jnp.concatenate([a, eye], axis=1)
    done = []
    top = 0
    for j in range(LEAF - 1):
        if j - top == 8:
            done.append(m[:8])
            m = m[8:]
            top = j
        row = m[j - top : j - top + 1]
        scaled = row * (1.0 / row[:, j : j + 1])
        below = lax.broadcasted_iota(jnp.int32, (LEAF - top, 1), 0) > j - top
        m = m - jnp.where(below, m[:, j : j + 1], 0.0) * scaled
    m = jnp.concatenate(done + [m], axis=0)
    pivot = jnp.sum(jnp.where(lane_id == row_id, m, 0.0), axis=1, keepdims=True)
    return m[:, LEAF:] * (1.0 / jnp.sqrt(pivot))


def block_inverse(a, size):
    if size == LEAF:
        return leaf_inverse(a)
    h = size // 2
    w11 = block_inverse(a[:h, :h], h)
    l21 = matmul_nt(a[h:, :h], w11)
    w22 = block_inverse(a[h:, h:] - matmul_nt(l21, l21), h)
    w21 = -matmul(w22, matmul(l21, w11))
    upper = jnp.concatenate([w11, jnp.zeros((h, h), F32)], axis=1)
    return jnp.concatenate([upper, jnp.concatenate([w21, w22], axis=1)], axis=0)


def kernel(
    order_ref, grad_ref, old_ref, sketches_ref, out_ref, fresh_ref,
    send_g, pair_g, pair_p, partial_y, own_y, total_y, recv_x, recv_y,
    part_s, recv_core, piece_s, recv_s, full_s,
    gram_part, gram_x, gram_y, gram_z, gram_full,
    core_sem, hi_sem, hi_gather_sem, gx_sem, gy_sem, gz_sem, gather_sem,
    g_sem, p_sem, fresh_sem, x_sem, y_sem,
):
    dp, tensor = lax.axis_index("dp"), lax.axis_index("tensor")
    z, y, x = dp // 16, (dp // 4) % 4, dp % 4
    hi, core = tensor // 2, tensor % 2

    across_z = ((1 - z) * 16 + y * 4 + x, tensor)
    across_core = (dp, hi * 2 + 1 - core)
    across_both = ((1 - z) * 16 + y * 4 + x, hi * 2 + 1 - core)

    def x_at(step):
        return (x + step) % 4

    def y_at(step):
        return (y + step) % 4

    def hi_at(step):
        return (hi + step) % 4

    def to_x(step):
        return (z * 16 + y * 4 + x_at(step), tensor)

    def to_y(step):
        return (z * 16 + y_at(step) * 4 + x, tensor)

    def to_hi(step):
        return (dp, hi_at(step) * 2 + core)

    def send(src, dst, sems, index, device):
        copy = pltpu.make_async_remote_copy(
            src_ref=src, dst_ref=dst, send_sem=sems.at[(0,) + index], recv_sem=sems.at[(1,) + index],
            device_id=device, device_id_type=MESH,
        )
        copy.start()
        return copy

    partners = [across_z, across_core, across_both]
    partners += [to(step) for to in (to_x, to_y, to_hi) for step in (1, 2, 3)]
    barrier = pltpu.get_barrier_semaphore()
    for device in partners:
        pl.semaphore_signal(barrier, inc=1, device_id=device, device_id_type=MESH)

    waits = []

    def sketch_partial(k):
        layer = order_ref[k]
        part_s[k] = jnp.zeros((ROWS, RANK), F32)

        @pl.loop(0, COLS // 512)
        def _(i):
            at = pl.ds(pl.multiple_of(i * 512, 512), 512)
            part_s[k] += jnp.dot(grad_ref[layer, :, at], sketches_ref[k, at, :], preferred_element_type=F32)

    sketch_partial(0)
    sketch_partial(1)
    pl.semaphore_wait(barrier, len(partners))
    core_copy = send(part_s.at[1 - core], recv_core, core_sem, (), across_core)

    def swap_columns(p):
        layer = order_ref[p]
        mine = pl.ds(pl.multiple_of(z * HALF, 128), HALF)
        other = pl.ds(pl.multiple_of((1 - z) * HALF, 128), HALF)

        @pl.loop(0, ROWS // 16)
        def _(i):
            at = pl.ds(pl.multiple_of(i * 16, 16), 16)
            send_g[p, at, :] = grad_ref[layer, at, other]
            pair_g[p, at, :] = grad_ref[layer, at, mine]

        copy = send(send_g.at[p], pair_g.at[p, pl.ds(ROWS, ROWS)], g_sem, (p,), across_z)
        waits.append(copy.wait_send)
        return copy

    def swap_old(p):
        pair_p[p, pl.ds(0, ROWS), :] = old_ref[order_ref[p]]
        copy = send(pair_p.at[p, pl.ds(0, ROWS)], pair_p.at[p, pl.ds(ROWS, ROWS)], p_sem, (p,), across_z)
        waits.append(copy.wait_send)
        return copy

    p_copies = {p: swap_old(p) for p in range(FRESH, LAYERS)}
    g_copies = {2: swap_columns(2)}

    core_copy.wait()
    for q in range(4):
        rows, lanes = pl.ds((q // 2) * 72, 72), pl.ds((q % 2) * 128, 128)
        piece_s[q] = part_s[core, rows, lanes] + recv_core[rows, lanes]
    recv_s[hi] = piece_s[hi]
    hi_copies = [
        send(piece_s.at[hi_at(s)], recv_s.at[hi], hi_sem, (s - 1,), to_hi(s)) for s in (1, 2, 3)
    ]
    g_copies[3] = swap_columns(3)
    for copy in hi_copies:
        copy.wait()
    full_s[hi] = (recv_s[0] + recv_s[1]) + (recv_s[2] + recv_s[3])
    hi_copies = [
        send(full_s.at[hi], full_s.at[hi], hi_gather_sem, (s - 1,), to_hi(s)) for s in (1, 2, 3)
    ]
    for copy in hi_copies:
        copy.wait()

    def whole_sketch():
        return jnp.concatenate(
            [
                jnp.concatenate([full_s[0], full_s[1]], axis=1),
                jnp.concatenate([full_s[2], full_s[3]], axis=1),
            ],
            axis=0,
        )

    sketch = whole_sketch()
    gram_part[...] = lax.dot_general(
        sketch, sketch, (((0,), (0,)), ((), ())), precision=HIGHEST, preferred_element_type=F32
    )
    gram_x[x] = gram_part[pl.ds(pl.multiple_of(x * 64, 64), 64), :]
    copies = [
        send(
            gram_part.at[pl.ds(pl.multiple_of(x_at(s) * 64, 64), 64)], gram_x.at[x], gx_sem, (s - 1,), to_x(s)
        )
        for s in (1, 2, 3)
    ]
    for copy in copies:
        copy.wait()
    gram_y[y] = (gram_x[0] + gram_x[1]) + (gram_x[2] + gram_x[3])
    copies = [send(gram_y.at[y], gram_y.at[y], gy_sem, (s - 1,), to_y(s)) for s in (1, 2, 3)]
    for copy in copies:
        copy.wait()
    gram_z[z] = (gram_y[0] + gram_y[1]) + (gram_y[2] + gram_y[3])
    send(gram_z.at[z], gram_z.at[z], gz_sem, (), across_z).wait()
    mine = pl.ds(pl.multiple_of(x * 64, 64), 64)
    gram_full[mine, :] = gram_z[0] + gram_z[1]
    copies = [send(gram_full.at[mine], gram_full.at[mine], gather_sem, (s - 1,), to_x(s)) for s in (1, 2, 3)]
    for copy in copies:
        copy.wait()

    x_copies, y_copies = {}, {}

    def project(p):
        x_copies[p] = []
        for half in range(2):
            at = pl.ds(half * (HALF // 2), HALF // 2)
            value = lax.dot_general(
                pair_g[p, :, at], pair_p[p], (((0,), (0,)), ((), ())), preferred_element_type=F32
            )
            own_y[...] = value.reshape(2, 4, ROWS, RANK)
            partial_y[p, pl.ds(2 * half, 2)] = own_y[...].astype(BF16)
            for row in range(2):
                total_y[p, 2 * half + row] = own_y[row, x]
            x_copies[p] += [
                send(
                    partial_y.at[p, pl.ds(2 * half, 2), x_at(s)], recv_x.at[p, s - 1, pl.ds(2 * half, 2)],
                    x_sem, (p, half, s - 1), to_x(s),
                )
                for s in (1, 2, 3)
            ]

    def sum_x(p):
        for copy in x_copies[p]:
            copy.wait()
        for row in range(4):
            total_y[p, row] += (
                recv_x[p, 0, row].astype(F32) + recv_x[p, 1, row].astype(F32) + recv_x[p, 2, row].astype(F32)
            )
        y_copies[p] = [
            send(total_y.at[p, y_at(s)], recv_y.at[p, s - 1], y_sem, (p, s - 1), to_y(s)) for s in (1, 2, 3)
        ]

    def sum_y(p):
        for copy in y_copies[p]:
            copy.wait()
        out_ref[p] = (total_y[p, y] + recv_y[p, 0]) + (recv_y[p, 1] + recv_y[p, 2])

    def project_old(p):
        g_copies[p].wait_recv()
        p_copies[p].wait_recv()
        project(p)

    project_old(2)
    g_copies[4] = swap_columns(4)
    g_copies[0] = swap_columns(0)
    project_old(3)
    g_copies[1] = swap_columns(1)

    inverse = block_inverse(gram_full[...], RANK)
    pair_p[core, pl.ds(0, ROWS), :] = matmul_nt(whole_sketch(), inverse).astype(BF16)
    mine = pair_p.at[core, pl.ds(0, ROWS)]
    theirs = pair_p.at[core, pl.ds(ROWS, ROWS)]
    fresh_copies = [
        send(mine, mine, fresh_sem, (0,), across_core),
        send(mine, theirs, fresh_sem, (1,), across_z),
        send(mine, theirs, fresh_sem, (2,), across_both),
    ]
    project_old(4)
    sum_x(2)
    sum_x(3)
    for copy in fresh_copies:
        copy.wait()
    for p in range(FRESH):
        g_copies[p].wait_recv()
        project(p)
    fresh_ref[...] = pair_p[pl.ds(0, FRESH), pl.ds(0, ROWS), :]
    sum_x(4)
    sum_y(2)
    sum_y(3)
    sum_x(0)
    sum_y(4)
    sum_x(1)
    sum_y(0)
    sum_y(1)
    for wait in waits:
        wait()


def per_device(gradients, old_projectors, sketches, refresh_order):
    dma = pltpu.SemaphoreType.DMA
    vmem = pltpu.VMEM
    by_position, fresh = pl.pallas_call(
        kernel,
        out_shape=(
            jax.ShapeDtypeStruct((LAYERS, ROWS, RANK), F32),
            jax.ShapeDtypeStruct((FRESH, ROWS, RANK), BF16),
        ),
        in_specs=[pl.BlockSpec(memory_space=pltpu.SMEM)] + [pl.BlockSpec(memory_space=vmem)] * 3,
        out_specs=(pl.BlockSpec(memory_space=vmem), pl.BlockSpec(memory_space=vmem)),
        scratch_shapes=[
            vmem((LAYERS, ROWS, HALF), BF16),
            vmem((LAYERS, 2 * ROWS, HALF), BF16),
            vmem((LAYERS, 2 * ROWS, RANK), BF16),
            vmem((LAYERS, 4, 4, ROWS, RANK), BF16),
            vmem((2, 4, ROWS, RANK), F32),
            vmem((LAYERS, 4, ROWS, RANK), F32),
            vmem((LAYERS, 3, 4, ROWS, RANK), BF16),
            vmem((LAYERS, 3, ROWS, RANK), F32),
            vmem((FRESH, ROWS, RANK), F32),
            vmem((ROWS, RANK), F32),
            vmem((4, 72, 128), F32),
            vmem((4, 72, 128), F32),
            vmem((4, 72, 128), F32),
            vmem((RANK, RANK), F32),
            vmem((4, 64, RANK), F32),
            vmem((4, 64, RANK), F32),
            vmem((2, 64, RANK), F32),
            vmem((RANK, RANK), F32),
            dma((2,)),
            dma((2, 3)),
            dma((2, 3)),
            dma((2, 3)),
            dma((2, 3)),
            dma((2,)),
            dma((2, 3)),
            dma((2, LAYERS)),
            dma((2, LAYERS)),
            dma((2, 3)),
            dma((2, LAYERS, 2, 3)),
            dma((2, LAYERS, 3)),
        ],
        compiler_params=pltpu.CompilerParams(
            collective_id=0, has_side_effects=True, vmem_limit_bytes=60 * 1024 * 1024
        ),
        cost_estimate=pl.CostEstimate(flops=2_400_000_000, bytes_accessed=13_000_000, transcendentals=0),
    )(refresh_order, gradients, old_projectors, sketches)
    position = jnp.arange(LAYERS, dtype=jnp.int32)
    place = jnp.sum(jnp.where(refresh_order[None, :] == position[:, None], position[None, :], 0), axis=1)
    return jnp.take(by_position, place, axis=0, mode="clip"), fresh


def solution(mesh):
    placed = (P(None, "dp", "tensor"), P(None, "dp", None), P(None, "tensor", None), P())
    return jax.shard_map(
        per_device,
        mesh=mesh,
        in_specs=placed,
        out_specs=(P(None, ("tensor", "dp"), None), P(None, "dp", None)),
        check_vma=False,
    )
```

```python
import jax
import jax.numpy as jnp
from jax import lax
from jax.experimental import pallas as pl
from jax.experimental.pallas import tpu as pltpu
from jax.sharding import PartitionSpec as P

MESH = pl.DeviceIdType.MESH
HIGHEST = lax.Precision.HIGHEST
F32 = jnp.float32
BF16 = jnp.bfloat16

ROWS = 144
COLS = 4608
HALF = COLS // 2
RANK = 256
LAYERS = 5
FRESH = 2
LEAF = 128
GROUP = 8
OLD = LAYERS - FRESH
WIDE = 640


def matmul(a, b):
    return jnp.dot(a, b, precision=HIGHEST, preferred_element_type=F32)


def matmul_nt(a, b):
    return lax.dot_general(a, b, (((1,), (1,)), ((), ())), precision=HIGHEST, preferred_element_type=F32)


def leaf_inverse(a):
    width = 2 * LEAF
    row_id = lax.broadcasted_iota(jnp.int32, (LEAF, width), 0)
    lane_id = lax.broadcasted_iota(jnp.int32, (LEAF, width), 1)
    eye = (lane_id[:, :LEAF] == row_id[:, :LEAF]).astype(F32)
    m = jnp.concatenate([a, eye], axis=1)
    done = []
    for j in range(0, LEAF, GROUP):
        if j:
            done.append(m[:GROUP])
            m = m[GROUP:]
        rows = [m[q : q + 1] for q in range(GROUP)]
        s = [[jnp.broadcast_to(rows[q][:, j + r : j + r + 1], (1, width)) for r in range(GROUP)] for q in range(GROUP)]
        factor = [[None] * GROUP for _ in range(GROUP)]
        inverse = []
        for q in range(GROUP):
            inverse.append(1.0 / s[q][q])
            for r in range(q + 1, GROUP):
                factor[r][q] = s[q][r] * inverse[q]
            for r in range(q + 1, GROUP):
                for t in range(r, GROUP):
                    s[r][t] = s[r][t] - factor[r][q] * s[q][t]
        upper, column = [], []
        below = row_id[: LEAF - j]
        for q in range(GROUP):
            u, c = rows[q], jnp.broadcast_to(m[:, j + q : j + q + 1], m.shape)
            if q == 0:
                start = m
            for r in range(q):
                u = u - factor[q][r] * upper[r]
                c = c - factor[q][r] * column[r]
            upper.append(u)
            column.append(c)
            start = start - jnp.where(below > q, c, 0.0) * (u * inverse[q])
        m = start
    m = jnp.concatenate(done + [m], axis=0)
    pivot = jnp.sum(jnp.where(lane_id == row_id, m, 0.0), axis=1, keepdims=True)
    return m[:, LEAF:] * (1.0 / jnp.sqrt(pivot))


def kernel(
    order_ref, grad_ref, old_ref, sketches_ref, out_ref, fresh_ref,
    own_g, quad_g, quad_s, quad_p, wide_y, partial_a, total_a, recv_xa, recv_z,
    send_g, pair_g, pair_p, partial_y, own_y, total_y, recv_x, recv_y,
    part_s, recv_core, piece_s, recv_s, full_s,
    gram_part, gram_x, gram_y, gram_z, gram_full,
    core_sem, hi_sem, hi_gather_sem, gx_sem, gy_sem, gz_sem, gather_sem,
    quad_sem, quad_s_sem, fresh_sem, xa_sem, za_sem, g_sem, p_sem, x_sem, y_sem,
):
    dp, tensor = lax.axis_index("dp"), lax.axis_index("tensor")
    z, y, x = dp // 16, (dp // 4) % 4, dp % 4
    hi, core = tensor // 2, tensor % 2

    across_z = ((1 - z) * 16 + y * 4 + x, tensor)
    across_core = (dp, hi * 2 + 1 - core)

    def x_at(step):
        return (x + step) % 4

    def y_at(step):
        return (y + step) % 4

    def hi_at(step):
        return (hi + step) % 4

    def to_x(step):
        return (z * 16 + y * 4 + x_at(step), tensor)

    def to_y(step):
        return (z * 16 + y_at(step) * 4 + x, tensor)

    def to_hi(step):
        return (dp, hi_at(step) * 2 + core)

    started = []

    def send(src, dst, sems, index, device):
        copy = pltpu.make_async_remote_copy(
            src_ref=src, dst_ref=dst, send_sem=sems.at[(0,) + index], recv_sem=sems.at[(1,) + index],
            device_id=device, device_id_type=MESH,
        )
        copy.start()
        started.append(copy)
        return copy

    def received(copies):
        for copy in copies:
            copy.wait_recv()

    partners = [across_z, across_core]
    partners += [to(step) for to in (to_x, to_y, to_hi) for step in (1, 2, 3)]
    barrier = pltpu.get_barrier_semaphore()
    for device in partners:
        pl.semaphore_signal(barrier, inc=1, device_id=device, device_id_type=MESH)

    for k in range(FRESH):
        part_s[k] = jnp.zeros((ROWS, RANK), F32)

        @pl.loop(0, COLS // 512)
        def _(i):
            at = pl.ds(pl.multiple_of(i * 512, 512), 512)
            part_s[k] += jnp.dot(grad_ref[order_ref[k], :, at], sketches_ref[k, at, :], preferred_element_type=F32)

    pl.semaphore_wait(barrier, len(partners))
    core_copy = send(part_s.at[1 - core], recv_core, core_sem, (), across_core)

    def window(y_of, z_of):
        return pl.ds(pl.multiple_of(z_of * HALF + y_of * 576 - 64 * (y_of % 2), 128), WIDE)

    quad_copies = {}

    def gather_rows(k):
        @pl.loop(0, ROWS // 16)
        def _(i):
            at = pl.ds(pl.multiple_of(i * 16, 16), 16)
            own_g[k, at, :] = grad_ref[order_ref[k], at, :]
            for half in range(2):
                quad_g[k, half, at, :] = grad_ref[order_ref[k], at, window(y, half)]

        quad_copies[k] = [
            send(
                own_g.at[k, :, window(y_at(s), half)], quad_g.at[k, half, pl.ds(s * ROWS, ROWS)],
                quad_sem, (k, half, s - 1), to_y(s),
            )
            for half in range(2)
            for s in (1, 2, 3)
        ]

    def split_columns(p):
        mine, other = z * HALF, (1 - z) * HALF

        @pl.loop(0, ROWS // 16)
        def _(i):
            at = pl.ds(pl.multiple_of(i * 16, 16), 16)
            send_g[p, at, :] = grad_ref[order_ref[p + FRESH], at, pl.ds(pl.multiple_of(other, 128), HALF)]
            pair_g[p, at, :] = grad_ref[order_ref[p + FRESH], at, pl.ds(pl.multiple_of(mine, 128), HALF)]

        pair_p[p, pl.ds(0, ROWS), :] = old_ref[order_ref[p + FRESH]]

    g_copies, p_copies, x_copies, y_copies, xa_copies, za_copies = {}, {}, {}, {}, {}, {}

    def part(half):
        return pl.ds(half * (HALF // 2), HALF // 2)

    def swap(p, half):
        if half == 0:
            p_copies[p] = send(
                pair_p.at[p, pl.ds(0, ROWS)], pair_p.at[p, pl.ds(ROWS, ROWS)], p_sem, (p,), across_z
            )
        g_copies[p, half] = send(
            send_g.at[p, :, part(half)], pair_g.at[p, pl.ds(ROWS, ROWS), part(half)], g_sem, (p, half), across_z
        )

    def project_old(p, half):
        received([g_copies[p, half]] + ([p_copies[p]] if half == 0 else []))
        value = lax.dot_general(
            pair_g[p, :, part(half)], pair_p[p], (((0,), (0,)), ((), ())), preferred_element_type=F32
        )
        own_y[...] = value.reshape(2, 4, ROWS, RANK)
        partial_y[p, pl.ds(2 * half, 2)] = own_y[...].astype(BF16)
        for row in range(2):
            total_y[p, 2 * half + row] = own_y[row, x]
        x_copies[p, half] = [
            send(
                partial_y.at[p, pl.ds(2 * half, 2), x_at(s)], recv_x.at[p, s - 1, pl.ds(2 * half, 2)],
                x_sem, (p, half, s - 1), to_x(s),
            )
            for s in (1, 2, 3)
        ]

    def sum_x_old(p):
        for half in range(2):
            received(x_copies[p, half])
        for row in range(4):
            total_y[p, row] += (
                recv_x[p, 0, row].astype(F32) + recv_x[p, 1, row].astype(F32) + recv_x[p, 2, row].astype(F32)
            )
        y_copies[p] = [
            send(total_y.at[p, y_at(s)], recv_y.at[p, s - 1], y_sem, (p, s - 1), to_y(s)) for s in (1, 2, 3)
        ]

    def finish_old(p):
        received(y_copies[p])
        out_ref[p + FRESH] = (total_y[p, y] + recv_y[p, 0]) + (recv_y[p, 1] + recv_y[p, 2])

    def project_fresh(k):
        received(quad_copies[k])
        for half in range(2):
            wide_y[...] = lax.dot_general(
                quad_g[k, half], quad_p[k], (((0,), (0,)), ((), ())), preferred_element_type=F32
            )
            first = 64 * (y % 2)
            for column in range(4):
                partial_a[k, half, column] = wide_y[
                    pl.ds(pl.multiple_of(first + column * ROWS, 16), ROWS), :
                ].astype(BF16)
            total_a[k, half] = wide_y[pl.ds(pl.multiple_of(first + x * ROWS, 16), ROWS), :]
        xa_copies[k] = [
            send(partial_a.at[k, :, x_at(s)], recv_xa.at[k, s - 1], xa_sem, (k, s - 1), to_x(s)) for s in (1, 2, 3)
        ]

    def sum_x_fresh(k):
        received(xa_copies[k])
        for half in range(2):
            total_a[k, half] += (
                recv_xa[k, 0, half].astype(F32) + recv_xa[k, 1, half].astype(F32) + recv_xa[k, 2, half].astype(F32)
            )
        za_copies[k] = send(total_a.at[k, 1 - z], recv_z.at[k], za_sem, (k,), across_z)

    def finish_fresh(k):
        received([za_copies[k]])
        out_ref[k] = total_a[k, z] + recv_z[k]

    gather_rows(0)
    received([core_copy])
    for q in range(4):
        rows, lanes = pl.ds((q // 2) * 72, 72), pl.ds((q % 2) * 128, 128)
        piece_s[q] = part_s[core, rows, lanes] + recv_core[rows, lanes]
    recv_s[hi] = piece_s[hi]
    copies = [send(piece_s.at[hi_at(s)], recv_s.at[hi], hi_sem, (s - 1,), to_hi(s)) for s in (1, 2, 3)]
    split_columns(0)
    split_columns(1)
    received(copies)
    full_s[hi] = (recv_s[0] + recv_s[1]) + (recv_s[2] + recv_s[3])
    copies = [send(full_s.at[hi], full_s.at[hi], hi_gather_sem, (s - 1,), to_hi(s)) for s in (1, 2, 3)]
    swap(0, 0)
    split_columns(2)
    received(copies)

    quad_s[0] = jnp.concatenate(
        [
            jnp.concatenate([full_s[0], full_s[1]], axis=1),
            jnp.concatenate([full_s[2], full_s[3]], axis=1),
        ],
        axis=0,
    )
    sketch = quad_s[0]
    gram_part[...] = lax.dot_general(
        sketch, sketch, (((0,), (0,)), ((), ())), precision=HIGHEST, preferred_element_type=F32
    )
    gram_x[x] = gram_part[pl.ds(pl.multiple_of(x * 64, 64), 64), :]
    copies = [
        send(
            gram_part.at[pl.ds(pl.multiple_of(x_at(s) * 64, 64), 64)], gram_x.at[x], gx_sem, (s - 1,), to_x(s)
        )
        for s in (1, 2, 3)
    ]
    swap(0, 1)
    received(copies)
    gram_y[y] = (gram_x[0] + gram_x[1]) + (gram_x[2] + gram_x[3])
    copies = [send(gram_y.at[y], gram_y.at[y], gy_sem, (s - 1,), to_y(s)) for s in (1, 2, 3)]
    project_old(0, 0)
    received(copies)
    gram_z[z] = (gram_y[0] + gram_y[1]) + (gram_y[2] + gram_y[3])
    copies = [send(gram_z.at[z], gram_z.at[z], gz_sem, (), across_z)]
    quad_s_copies = [send(quad_s.at[0], quad_s.at[s], quad_s_sem, (s - 1,), to_y(s)) for s in (1, 2, 3)]
    swap(1, 0)
    gather_rows(1)
    received(copies)
    mine = pl.ds(pl.multiple_of(x * 64, 64), 64)
    gram_full[mine, :] = gram_z[0] + gram_z[1]
    copies = [send(gram_full.at[mine], gram_full.at[mine], gather_sem, (s - 1,), to_x(s)) for s in (1, 2, 3)]
    project_old(0, 1)
    received(copies)

    swap(1, 1)
    w11 = leaf_inverse(gram_full[pl.ds(0, LEAF), pl.ds(0, LEAF)])
    l21 = matmul_nt(gram_full[pl.ds(LEAF, LEAF), pl.ds(0, LEAF)], w11)
    project_old(1, 0)
    swap(2, 0)
    w22 = leaf_inverse(gram_full[pl.ds(LEAF, LEAF), pl.ds(LEAF, LEAF)] - matmul_nt(l21, l21))
    w21 = -matmul(w22, matmul(l21, w11))
    swap(2, 1)
    received(quad_s_copies)
    whole = quad_s[...].reshape(4 * ROWS, RANK)
    left = matmul_nt(whole[:, :LEAF], w11)
    right = matmul_nt(whole[:, :LEAF], w21) + matmul_nt(whole[:, LEAF:], w22)
    quad_p[core] = jnp.concatenate([left, right], axis=1).astype(BF16)
    fresh_copy = send(quad_p.at[core], quad_p.at[core], fresh_sem, (), across_core)
    project_old(1, 1)
    sum_x_old(0)
    received([fresh_copy])
    fresh_ref[...] = quad_p[:, pl.ds(0, ROWS), :]
    project_fresh(0)
    project_fresh(1)
    project_old(2, 0)
    project_old(2, 1)
    sum_x_old(1)
    finish_old(0)
    sum_x_fresh(0)
    sum_x_fresh(1)
    finish_old(1)
    sum_x_old(2)
    finish_fresh(0)
    finish_fresh(1)
    finish_old(2)
    for copy in started:
        copy.wait_send()


def place(order_ref, by_position_ref, fresh_ref, out_ref, fresh_out_ref):
    for p in range(LAYERS):
        out_ref[order_ref[p]] = by_position_ref[p]
    fresh_out_ref[...] = fresh_ref[...]


def per_device(gradients, old_projectors, sketches, refresh_order):
    dma = pltpu.SemaphoreType.DMA
    vmem = pltpu.VMEM
    shapes = (
        jax.ShapeDtypeStruct((LAYERS, ROWS, RANK), F32),
        jax.ShapeDtypeStruct((FRESH, ROWS, RANK), BF16),
    )
    smem = pl.BlockSpec(memory_space=pltpu.SMEM)
    whole = pl.BlockSpec(memory_space=vmem)
    by_position, fresh = pl.pallas_call(
        kernel,
        out_shape=shapes,
        in_specs=[smem] + [whole] * 3,
        out_specs=(whole, whole),
        scratch_shapes=[
            vmem((FRESH, ROWS, COLS), BF16),
            vmem((FRESH, 2, 4 * ROWS, WIDE), BF16),
            vmem((4, ROWS, RANK), F32),
            vmem((FRESH, 4 * ROWS, RANK), BF16),
            vmem((WIDE, RANK), F32),
            vmem((FRESH, 2, 4, ROWS, RANK), BF16),
            vmem((FRESH, 2, ROWS, RANK), F32),
            vmem((FRESH, 3, 2, ROWS, RANK), BF16),
            vmem((FRESH, ROWS, RANK), F32),
            vmem((OLD, ROWS, HALF), BF16),
            vmem((OLD, 2 * ROWS, HALF), BF16),
            vmem((OLD, 2 * ROWS, RANK), BF16),
            vmem((OLD, 4, 4, ROWS, RANK), BF16),
            vmem((2, 4, ROWS, RANK), F32),
            vmem((OLD, 4, ROWS, RANK), F32),
            vmem((OLD, 3, 4, ROWS, RANK), BF16),
            vmem((OLD, 3, ROWS, RANK), F32),
            vmem((FRESH, ROWS, RANK), F32),
            vmem((ROWS, RANK), F32),
            vmem((4, 72, 128), F32),
            vmem((4, 72, 128), F32),
            vmem((4, 72, 128), F32),
            vmem((RANK, RANK), F32),
            vmem((4, 64, RANK), F32),
            vmem((4, 64, RANK), F32),
            vmem((2, 64, RANK), F32),
            vmem((RANK, RANK), F32),
            dma((2,)),
            dma((2, 3)),
            dma((2, 3)),
            dma((2, 3)),
            dma((2, 3)),
            dma((2,)),
            dma((2, 3)),
            dma((2, FRESH, 2, 3)),
            dma((2, 3)),
            dma((2,)),
            dma((2, FRESH, 3)),
            dma((2, FRESH)),
            dma((2, OLD, 2)),
            dma((2, OLD)),
            dma((2, OLD, 2, 3)),
            dma((2, OLD, 3)),
        ],
        compiler_params=pltpu.CompilerParams(
            collective_id=0, has_side_effects=True, vmem_limit_bytes=60 * 1024 * 1024
        ),
        cost_estimate=pl.CostEstimate(flops=2_400_000_000, bytes_accessed=13_000_000, transcendentals=0),
    )(refresh_order, gradients, old_projectors, sketches)
    return pl.pallas_call(
        place,
        out_shape=shapes,
        in_specs=[smem, whole, whole],
        out_specs=(whole, whole),
        cost_estimate=pl.CostEstimate(flops=0, bytes_accessed=1_800_000, transcendentals=0),
    )(refresh_order, by_position, fresh)


def solution(mesh):
    placed = (P(None, "dp", "tensor"), P(None, "dp", None), P(None, "tensor", None), P())
    return jax.shard_map(
        per_device,
        mesh=mesh,
        in_specs=placed,
        out_specs=(P(None, ("tensor", "dp"), None), P(None, "dp", None)),
        check_vma=False,
    )
```

```python
import jax
import jax.numpy as jnp
from jax import lax
from jax.experimental import pallas as pl
from jax.experimental.pallas import tpu as pltpu
from jax.sharding import PartitionSpec as P

MESH = pl.DeviceIdType.MESH
HIGHEST = lax.Precision.HIGHEST
F32 = jnp.float32
BF16 = jnp.bfloat16

ROWS = 144
COLS = 4608
HALF = COLS // 2
RANK = 256
LAYERS = 5
FRESH = 2
LEAF = 128
GROUP = 8
OLD = 2
WIDE = 640


def matmul(a, b):
    return jnp.dot(a, b, precision=HIGHEST, preferred_element_type=F32)


def matmul_nt(a, b):
    return lax.dot_general(a, b, (((1,), (1,)), ((), ())), precision=HIGHEST, preferred_element_type=F32)


def leaf_inverse(a):
    width = 2 * LEAF
    row_id = lax.broadcasted_iota(jnp.int32, (LEAF, width), 0)
    lane_id = lax.broadcasted_iota(jnp.int32, (LEAF, width), 1)
    eye = (lane_id[:, :LEAF] == row_id[:, :LEAF]).astype(F32)
    m = jnp.concatenate([a, eye], axis=1)
    done = []
    for j in range(0, LEAF, GROUP):
        if j:
            done.append(m[:GROUP])
            m = m[GROUP:]
        rows = [m[q : q + 1] for q in range(GROUP)]
        s = [[jnp.broadcast_to(rows[q][:, j + r : j + r + 1], (1, width)) for r in range(GROUP)] for q in range(GROUP)]
        factor = [[None] * GROUP for _ in range(GROUP)]
        inverse = []
        for q in range(GROUP):
            inverse.append(1.0 / s[q][q])
            for r in range(q + 1, GROUP):
                factor[r][q] = s[q][r] * inverse[q]
            for r in range(q + 1, GROUP):
                for t in range(r, GROUP):
                    s[r][t] = s[r][t] - factor[r][q] * s[q][t]
        upper, column = [], []
        below = row_id[: LEAF - j]
        for q in range(GROUP):
            u, c = rows[q], jnp.broadcast_to(m[:, j + q : j + q + 1], m.shape)
            if q == 0:
                start = m
            for r in range(q):
                u = u - factor[q][r] * upper[r]
                c = c - factor[q][r] * column[r]
            upper.append(u)
            column.append(c)
            start = start - jnp.where(below > q, c, 0.0) * (u * inverse[q])
        m = start
    m = jnp.concatenate(done + [m], axis=0)
    pivot = jnp.sum(jnp.where(lane_id == row_id, m, 0.0), axis=1, keepdims=True)
    return m[:, LEAF:] * (1.0 / jnp.sqrt(pivot))


def kernel(
    order_ref, grad_hbm, old_ref, sketches_hbm, out_ref, fresh_ref,
    grad_ref, sketches_ref,
    own_g, quad_g, quad_s, quad_p, wide_y, partial_a, total_a, recv_xa, recv_z,
    pack_g, ring_g, ring_p, partial_b, total_b, recv_yb, recv_zb,
    send_g, pair_g, pair_p, partial_y, own_y, total_y, recv_x, recv_y,
    part_s, recv_core, piece_s, recv_s, full_s,
    gram_part, gram_x, gram_y, gram_z, gram_full,
    load_sem, core_sem, hi_sem, hi_gather_sem, gx_sem, gy_sem, gz_sem, gather_sem,
    quad_sem, quad_s_sem, fresh_sem, xa_sem, za_sem, ring_sem, ring_p_sem, yb_sem, zb_sem, g_sem, p_sem, x_sem, y_sem,
):
    dp, tensor = lax.axis_index("dp"), lax.axis_index("tensor")
    z, y, x = dp // 16, (dp // 4) % 4, dp % 4
    hi, core = tensor // 2, tensor % 2

    across_z = ((1 - z) * 16 + y * 4 + x, tensor)
    across_core = (dp, hi * 2 + 1 - core)

    def x_at(step):
        return (x + step) % 4

    def y_at(step):
        return (y + step) % 4

    def hi_at(step):
        return (hi + step) % 4

    def to_x(step):
        return (z * 16 + y * 4 + x_at(step), tensor)

    def to_y(step):
        return (z * 16 + y_at(step) * 4 + x, tensor)

    def to_hi(step):
        return (dp, hi_at(step) * 2 + core)

    started = []

    def send(src, dst, sems, index, device):
        copy = pltpu.make_async_remote_copy(
            src_ref=src, dst_ref=dst, send_sem=sems.at[(0,) + index], recv_sem=sems.at[(1,) + index],
            device_id=device, device_id_type=MESH,
        )
        copy.start()
        started.append(copy)
        return copy

    def received(copies):
        for copy in copies:
            copy.wait_recv()

    partners = [across_z, across_core]
    partners += [to(step) for to in (to_x, to_y, to_hi) for step in (1, 2, 3)]
    barrier = pltpu.get_barrier_semaphore()
    for device in partners:
        pl.semaphore_signal(barrier, inc=1, device_id=device, device_id_type=MESH)

    loads = [
        pltpu.make_async_copy(grad_hbm, grad_ref, load_sem.at[0]),
        pltpu.make_async_copy(sketches_hbm, sketches_ref, load_sem.at[1]),
    ]
    for load in loads:
        load.start()

    def to_ring(step):
        return (z * 16 + (y + step * (1 - core)) % 4 * 4 + (x + step * core) % 4, tensor)

    def window(y_of, z_of):
        return pl.ds(pl.multiple_of(z_of * HALF + y_of * 576 - 64 * (y_of % 2), 128), WIDE)

    def gather_over_y():
        @pl.loop(0, ROWS // 16)
        def _(i):
            at = pl.ds(pl.multiple_of(i * 16, 16), 16)
            own_g[at, :] = grad_ref[order_ref[0], at, :]
            for half in range(2):
                quad_g[half, at, :] = grad_ref[order_ref[0], at, window(y, half)]

        return [
            send(
                own_g.at[:, window(y_at(s), half)], quad_g.at[half, pl.ds(s * ROWS, ROWS)],
                quad_sem, (half, s - 1), to_y(s),
            )
            for half in range(2)
            for s in (1, 2, 3)
        ]

    def project_over_y():
        for half in range(2):
            wide_y[...] = lax.dot_general(
                quad_g[half], quad_p[0], (((0,), (0,)), ((), ())), preferred_element_type=F32
            )
            first = 64 * (y % 2)
            for column in range(4):
                partial_a[half, column] = wide_y[
                    pl.ds(pl.multiple_of(first + column * ROWS, 16), ROWS), :
                ].astype(BF16)
            total_a[half] = wide_y[pl.ds(pl.multiple_of(first + x * ROWS, 16), ROWS), :]
        return [send(partial_a.at[:, x_at(s)], recv_xa.at[s - 1], xa_sem, (s - 1,), to_x(s)) for s in (1, 2, 3)]

    def sum_over_x(copies):
        received(copies)
        for half in range(2):
            total_a[half] += (
                recv_xa[0, half].astype(F32) + recv_xa[1, half].astype(F32) + recv_xa[2, half].astype(F32)
            )
        return send(total_a.at[1 - z], recv_z, za_sem, (), across_z)

    def pack_columns(a, position):
        @pl.loop(0, ROWS // 16)
        def _(i):
            at = pl.ds(pl.multiple_of(i * 16, 16), 16)
            for column in range(4):
                pieces = []
                for block in range(column, 32, 4):
                    start, stop = block * ROWS // 128 * 128, -(-(block + 1) * ROWS // 128) * 128
                    tiles = grad_ref[order_ref[position], at, pl.ds(start, stop - start)]
                    pieces.append(tiles[:, block * ROWS - start : (block + 1) * ROWS - start])
                pack_g[a, column, at, :] = jnp.concatenate(pieces, axis=1)

    def gather_over_x(a, steps):
        return [
            send(pack_g.at[a, x_at(s)], ring_g.at[a, pl.ds(s * ROWS, ROWS)], ring_sem, (a, s - 1), to_x(s))
            for s in steps
        ]

    def project_over_x(a, projector):
        ring_g[a, pl.ds(0, ROWS), :] = pack_g[a, x]
        value = lax.dot_general(ring_g[a], projector, (((0,), (0,)), ((), ())), preferred_element_type=F32)
        own_y[...] = value.reshape(2, 4, ROWS, RANK)
        partial_b[a] = own_y[...].astype(BF16)
        total_b[a] = own_y[:, y]
        return [
            send(partial_b.at[a, :, y_at(s)], recv_yb.at[a, s - 1], yb_sem, (a, s - 1), to_y(s)) for s in (1, 2, 3)
        ]

    def sum_over_y(a, copies):
        received(copies)
        for half in range(2):
            total_b[a, half] += (
                recv_yb[a, 0, half].astype(F32) + recv_yb[a, 1, half].astype(F32) + recv_yb[a, 2, half].astype(F32)
            )
        return send(total_b.at[a, 1 - z], recv_zb.at[a], zb_sem, (a,), across_z)

    def split_columns(p):
        mine, other = z * HALF, (1 - z) * HALF

        @pl.loop(0, ROWS // 16)
        def _(i):
            at = pl.ds(pl.multiple_of(i * 16, 16), 16)
            send_g[p, at, :] = grad_ref[order_ref[p + FRESH], at, pl.ds(pl.multiple_of(other, 128), HALF)]
            pair_g[p, at, :] = grad_ref[order_ref[p + FRESH], at, pl.ds(pl.multiple_of(mine, 128), HALF)]

        pair_p[p, pl.ds(0, ROWS), :] = old_ref[order_ref[p + FRESH]]

    def part(half):
        return pl.ds(half * (HALF // 2), HALF // 2)

    def swap(p, half):
        copies = []
        if half == 0:
            copies.append(
                send(pair_p.at[p, pl.ds(0, ROWS)], pair_p.at[p, pl.ds(ROWS, ROWS)], p_sem, (p,), across_z)
            )
        copies.append(
            send(
                send_g.at[p, :, part(half)], pair_g.at[p, pl.ds(ROWS, ROWS), part(half)],
                g_sem, (p, half), across_z,
            )
        )
        return copies

    def project_pair(p, half):
        value = lax.dot_general(
            pair_g[p, :, part(half)], pair_p[p], (((0,), (0,)), ((), ())), preferred_element_type=F32
        )
        own_y[...] = value.reshape(2, 4, ROWS, RANK)
        partial_y[p, pl.ds(2 * half, 2)] = own_y[...].astype(BF16)

    def project_y_first():
        for half in range(2):
            project_pair(0, half)

            @pl.when(y // 2 == half)
            def _():
                total_y[0] = own_y[y % 2]

        return [
            send(partial_y.at[0, y_at(s)], recv_x.at[0, s - 1], x_sem, (0, 0, s - 1), to_y(s)) for s in (1, 2, 3)
        ]

    def project_x_first(half):
        project_pair(1, half)
        for row in range(2):
            total_y[1, 2 * half + row] = own_y[row, x]
        return [
            send(
                partial_y.at[1, pl.ds(2 * half, 2), x_at(s)], recv_x.at[1, s - 1, pl.ds(2 * half, 2)],
                x_sem, (1, half, s - 1), to_x(s),
            )
            for s in (1, 2, 3)
        ]

    def sum_old(p, copies):
        received(copies)
        for row in range(4):
            total_y[p, row] += (
                recv_x[p, 0, row].astype(F32) + recv_x[p, 1, row].astype(F32) + recv_x[p, 2, row].astype(F32)
            )
        at, to = ((x_at, to_x), (y_at, to_y))[p]
        return [send(total_y.at[p, at(s)], recv_y.at[p, s - 1], y_sem, (p, s - 1), to(s)) for s in (1, 2, 3)]

    def finish_old(p, copies):
        received(copies)
        mine = (x, y)[p]
        out_ref[p + FRESH] = (total_y[p, mine] + recv_y[p, 0]) + (recv_y[p, 1] + recv_y[p, 2])

    def start():
        loads[0].wait()
        pack_columns(0, 1)
        pl.semaphore_wait(barrier, len(partners))

    def sketch_partials():
        loads[1].wait()
        for k in range(FRESH):
            part_s[k] = jnp.zeros((ROWS, RANK), F32)

            @pl.loop(0, COLS // 512)
            def _(i):
                at = pl.ds(pl.multiple_of(i * 512, 512), 512)
                part_s[k] += jnp.dot(
                    grad_ref[order_ref[k], :, at], sketches_ref[k, at, :], preferred_element_type=F32
                )

        return [send(part_s.at[1 - core], recv_core, core_sem, (), across_core)]

    def sketch_scatter(copies):
        received(copies)
        for q in range(4):
            rows, lanes = pl.ds((q // 2) * 72, 72), pl.ds((q % 2) * 128, 128)
            piece_s[q] = part_s[core, rows, lanes] + recv_core[rows, lanes]
        recv_s[hi] = piece_s[hi]
        return [send(piece_s.at[hi_at(s)], recv_s.at[hi], hi_sem, (s - 1,), to_hi(s)) for s in (1, 2, 3)]

    def sketch_gather(copies):
        received(copies)
        full_s[hi] = (recv_s[0] + recv_s[1]) + (recv_s[2] + recv_s[3])
        return [send(full_s.at[hi], full_s.at[hi], hi_gather_sem, (s - 1,), to_hi(s)) for s in (1, 2, 3)]

    def gram_over_x(copies):
        received(copies)
        quad_s[0] = jnp.concatenate(
            [
                jnp.concatenate([full_s[0], full_s[1]], axis=1),
                jnp.concatenate([full_s[2], full_s[3]], axis=1),
            ],
            axis=0,
        )
        sketch = quad_s[0]
        gram_part[...] = lax.dot_general(
            sketch, sketch, (((0,), (0,)), ((), ())), precision=HIGHEST, preferred_element_type=F32
        )
        gram_x[x] = gram_part[pl.ds(pl.multiple_of(x * 64, 64), 64), :]
        return [
            send(
                gram_part.at[pl.ds(pl.multiple_of(x_at(s) * 64, 64), 64)], gram_x.at[x],
                gx_sem, (s - 1,), to_x(s),
            )
            for s in (1, 2, 3)
        ]

    def gram_over_y(copies):
        received(copies)
        gram_y[y] = (gram_x[0] + gram_x[1]) + (gram_x[2] + gram_x[3])
        return [send(gram_y.at[y], gram_y.at[y], gy_sem, (s - 1,), to_y(s)) for s in (1, 2, 3)]

    def gram_over_z(copies):
        received(copies)
        gram_z[z] = (gram_y[0] + gram_y[1]) + (gram_y[2] + gram_y[3])
        return [send(gram_z.at[z], gram_z.at[z], gz_sem, (), across_z)]

    def gram_gather(copies):
        received(copies)
        mine = pl.ds(pl.multiple_of(x * 64, 64), 64)
        gram_full[mine, :] = gram_z[0] + gram_z[1]
        return [send(gram_full.at[mine], gram_full.at[mine], gather_sem, (s - 1,), to_x(s)) for s in (1, 2, 3)]

    def gather_sketch():
        return [send(quad_s.at[0], quad_s.at[s], quad_s_sem, (s - 1,), to_ring(s)) for s in (1, 2, 3)]

    def gather_old():
        ring_p[pl.ds(0, ROWS), :] = old_ref[order_ref[4]]
        return [
            send(ring_p.at[pl.ds(0, ROWS)], ring_p.at[pl.ds(s * ROWS, ROWS)], ring_p_sem, (s - 1,), to_x(s))
            for s in (1, 2, 3)
        ]

    def first_block(copies):
        received(copies)
        w11 = leaf_inverse(gram_full[pl.ds(0, LEAF), pl.ds(0, LEAF)])
        return w11, matmul_nt(gram_full[pl.ds(LEAF, LEAF), pl.ds(0, LEAF)], w11)

    def second_block(w11, l21):
        w22 = leaf_inverse(gram_full[pl.ds(LEAF, LEAF), pl.ds(LEAF, LEAF)] - matmul_nt(l21, l21))
        return -matmul(w22, matmul(l21, w11)), w22

    def project_sketch(copies, w11, w21, w22):
        received(copies)
        rows = quad_s[...].reshape(4 * ROWS, RANK)
        left = matmul_nt(rows[:, :LEAF], w11)
        right = matmul_nt(rows[:, :LEAF], w21) + matmul_nt(rows[:, LEAF:], w22)
        quad_p[core] = jnp.concatenate([left, right], axis=1).astype(BF16)
        return [send(quad_p.at[core], quad_p.at[core], fresh_sem, (), across_core)]

    start()
    f1 = gather_over_x(0, (1, 3))
    pack_columns(1, 4)
    last = gather_over_x(1, (1, 3))
    chain = sketch_partials()
    chain = sketch_scatter(chain)
    f0 = gather_over_y()
    split_columns(0)
    split_columns(1)
    chain = sketch_gather(chain)
    swap_0 = swap(0, 0)
    chain = gram_over_x(chain)
    last += gather_over_x(1, (2,))
    last += gather_old()
    chain = gram_over_y(chain)
    rows_s = gather_sketch()
    swap_0 += swap(0, 1)
    chain = gram_over_z(chain)
    swap_10 = swap(1, 0)
    received(swap_0)
    over_y_0 = project_y_first()
    chain = gram_gather(chain)
    f1 += gather_over_x(0, (2,))
    swap_11 = swap(1, 1)
    received(last)
    over_y_4 = project_over_x(1, ring_p[...])
    w11, l21 = first_block(chain)
    received(swap_10)
    over_x_1 = project_x_first(0)
    w21, w22 = second_block(w11, l21)
    received(swap_11)
    over_x_1 += project_x_first(1)
    chain = project_sketch(rows_s, w11, w21, w22)
    received(f1 + chain)
    over_y_f = project_over_x(0, quad_p[1])
    received(f0)
    over_x_f = project_over_y()
    fresh_ref[...] = quad_p[:, pl.ds(0, ROWS), :]
    last_0 = sum_old(0, over_y_0)
    last_4 = sum_over_y(1, over_y_4)
    last_1 = sum_old(1, over_x_1)
    last_f1 = sum_over_y(0, over_y_f)
    received([last_4])
    out_ref[4] = total_b[1, z] + recv_zb[1]
    last_f0 = sum_over_x(over_x_f)
    received([last_f1])
    out_ref[1] = total_b[0, z] + recv_zb[0]
    finish_old(0, last_0)
    finish_old(1, last_1)
    received([last_f0])
    out_ref[0] = total_a[z] + recv_z[...]
    for copy in started:
        copy.wait_send()


def place(order_ref, by_position_ref, fresh_ref, out_ref, fresh_out_ref):
    for p in range(LAYERS):
        out_ref[order_ref[p]] = by_position_ref[p]
    fresh_out_ref[...] = fresh_ref[...]


def per_device(gradients, old_projectors, sketches, refresh_order):
    dma = pltpu.SemaphoreType.DMA
    vmem = pltpu.VMEM
    shapes = (
        jax.ShapeDtypeStruct((LAYERS, ROWS, RANK), F32),
        jax.ShapeDtypeStruct((FRESH, ROWS, RANK), BF16),
    )
    smem = pl.BlockSpec(memory_space=pltpu.SMEM)
    whole = pl.BlockSpec(memory_space=vmem)
    anywhere = pl.BlockSpec(memory_space=pl.ANY)
    by_position, fresh = pl.pallas_call(
        kernel,
        out_shape=shapes,
        in_specs=[smem, anywhere, whole, anywhere],
        out_specs=(whole, whole),
        scratch_shapes=[
            vmem((LAYERS, ROWS, COLS), BF16),
            vmem((FRESH, COLS, RANK), BF16),
            vmem((ROWS, COLS), BF16),
            vmem((2, 4 * ROWS, WIDE), BF16),
            vmem((4, ROWS, RANK), F32),
            vmem((FRESH, 4 * ROWS, RANK), BF16),
            vmem((WIDE, RANK), F32),
            vmem((2, 4, ROWS, RANK), BF16),
            vmem((2, ROWS, RANK), F32),
            vmem((3, 2, ROWS, RANK), BF16),
            vmem((ROWS, RANK), F32),
            vmem((2, 4, ROWS, COLS // 4), BF16),
            vmem((2, 4 * ROWS, COLS // 4), BF16),
            vmem((4 * ROWS, RANK), BF16),
            vmem((2, 2, 4, ROWS, RANK), BF16),
            vmem((2, 2, ROWS, RANK), F32),
            vmem((2, 3, 2, ROWS, RANK), BF16),
            vmem((2, ROWS, RANK), F32),
            vmem((OLD, ROWS, HALF), BF16),
            vmem((OLD, 2 * ROWS, HALF), BF16),
            vmem((OLD, 2 * ROWS, RANK), BF16),
            vmem((OLD, 4, 4, ROWS, RANK), BF16),
            vmem((2, 4, ROWS, RANK), F32),
            vmem((OLD, 4, ROWS, RANK), F32),
            vmem((OLD, 3, 4, ROWS, RANK), BF16),
            vmem((OLD, 3, ROWS, RANK), F32),
            vmem((FRESH, ROWS, RANK), F32),
            vmem((ROWS, RANK), F32),
            vmem((4, 72, 128), F32),
            vmem((4, 72, 128), F32),
            vmem((4, 72, 128), F32),
            vmem((RANK, RANK), F32),
            vmem((4, 64, RANK), F32),
            vmem((4, 64, RANK), F32),
            vmem((2, 64, RANK), F32),
            vmem((RANK, RANK), F32),
            dma((2,)),
            dma((2,)),
            dma((2, 3)),
            dma((2, 3)),
            dma((2, 3)),
            dma((2, 3)),
            dma((2,)),
            dma((2, 3)),
            dma((2, 2, 3)),
            dma((2, 3)),
            dma((2,)),
            dma((2, 3)),
            dma((2,)),
            dma((2, 2, 3)),
            dma((2, 3)),
            dma((2, 2, 3)),
            dma((2, 2)),
            dma((2, OLD, 2)),
            dma((2, OLD)),
            dma((2, OLD, 2, 3)),
            dma((2, OLD, 3)),
        ],
        compiler_params=pltpu.CompilerParams(
            collective_id=0, has_side_effects=True, vmem_limit_bytes=60 * 1024 * 1024
        ),
        cost_estimate=pl.CostEstimate(flops=2_400_000_000, bytes_accessed=13_000_000, transcendentals=0),
    )(refresh_order, gradients, old_projectors, sketches)
    return pl.pallas_call(
        place,
        out_shape=shapes,
        in_specs=[smem, whole, whole],
        out_specs=(whole, whole),
        cost_estimate=pl.CostEstimate(flops=0, bytes_accessed=1_800_000, transcendentals=0),
    )(refresh_order, by_position, fresh)


def solution(mesh):
    placed = (P(None, "dp", "tensor"), P(None, "dp", None), P(None, "tensor", None), P())
    return jax.shard_map(
        per_device,
        mesh=mesh,
        in_specs=placed,
        out_specs=(P(None, ("tensor", "dp"), None), P(None, "dp", None)),
        check_vma=False,
    )
```
